512 devices in a mesh: sec: 128 (over z_hi, x, y, core), term: 4 (over z_lo).
Axes of the slice: x: 4, y: 8, z: 8 (z_hi: 2, z_lo: 4; z = z_hi * 4 + z_lo), core: 2. Of those that a mesh axis runs over, the one named last changes fastest.
Arguments:
- meet_env: bfloat16 [128, 24, 256, 256], P('sec', 'term'), may hold values from -0.375 to 0.375
- meet_iso: bfloat16 [128, 256, 2, 256], P('sec'), may hold values from -0.3125 to 0.3125
- last_site: bfloat16 [128, 256, 2, 256], P('sec'), may hold values from -60 to 60
- first_site: bfloat16 [128, 256, 2, 256], P('sec'), may hold values from -0.375 to 0.375
- term_kind: int32 [24, 2], P('term'), may hold values from 0 to 3
Outputs:
- two_site_out: float32 [128, 256, 2, 2, 256], P('sec')
The draws below stay inside these ranges and needn't reach their ends.
All inputs are finite; a program needn't handle non-finite values.
Results may differ from the reference program's by a relative error of at most 0.013.
Values may be sent and summed in bfloat16 or wider, within the bound.
No kernel may reach another device: no remote copies, remote signals or barrier semaphores. Data moves between devices by JAX's collectives and lax.ppermute only.
A program may use at most 64 MiB of HBM per device.

```python
import jax
import jax.numpy as jnp
import numpy as np
from jax import lax

BOND = 256
PHYS = 2
TERMS = 24
STEPS = 2
SECS = 128
N_TERM = 4


def draw_last_site(key, part):
    base_key, row_key = jax.random.split(key, 2)
    full_shape = (SECS, BOND, PHYS, BOND)
    base_draw = jax.random.truncated_normal(base_key, -6.0, 6.0, full_shape, jnp.float32)
    row_scale = 10.0 ** jax.random.uniform(row_key, (SECS, BOND, 1, 1), jnp.float32, 0.0, 1.0)
    return (base_draw * row_scale).astype(jnp.bfloat16)


def touch_ends(values, stream_key, smallest, top_value):
    shape = values.shape
    index_at = [jax.random.randint(jax.random.fold_in(stream_key, axis), (), 0, shape[axis]) for axis in range(len(shape))]
    values = values.at[tuple(index_at)].set(smallest)
    longest = shape.index(max(shape))
    index_at[longest] = (index_at[longest] + 1) % shape[longest]
    return values.at[tuple(index_at)].set(top_value)


def shard_levels(rng, extent, shards, low, largest):
    factor_of, own = 1.0, jax.random.fold_in(rng, 6)
    for axis_at, parts in shards:
        heights = jnp.exp(jax.random.uniform(jax.random.fold_in(own, axis_at), (parts,), jnp.float32, low / len(shards), largest / len(shards)))
        factor_of = factor_of * jnp.repeat(heights, extent[axis_at] // parts).reshape([-1 if axis == axis_at else 1 for axis in range(len(extent))])
    return factor_of


def bell_draw(rng, extent, scale, reach, shards=(), kind=jnp.bfloat16):
    drawn = jax.random.normal(rng, extent, jnp.float32) * scale
    if len(shards) > 0:
        drawn = shard_levels(rng, extent, shards, -0.22, 0.18) * drawn
    return jnp.clip(drawn, min=-reach, max=reach).astype(kind)


def setup_inputs(seed: int = 0) -> dict:
    key_list = jax.random.split(jax.random.key(seed), 6)
    meet_env = bell_draw(key_list[0], (SECS, TERMS, BOND, BOND), BOND ** -0.5, 0.375, ((0, 128), (1, 4)))
    meet_iso = bell_draw(key_list[1], (SECS, BOND, PHYS, BOND), (3 * BOND // 2) ** -0.5, 0.3125, ((0, 128),))
    last_site = draw_last_site(jax.random.fold_in(key_list[5], 71), 0)
    first_site = bell_draw(key_list[3], (SECS, BOND, PHYS, BOND), BOND ** -0.5, 0.375, ((0, 128),))
    term_kind = touch_ends(jax.random.randint(key_list[4], (TERMS, 2), 0, 4), jax.random.fold_in(key_list[4], 1), 0, 3).astype(jnp.int32)
    return dict(meet_env=meet_env, meet_iso=meet_iso, last_site=last_site, first_site=first_site, term_kind=term_kind)


operator_table = np.array([[[1.0, 0.0], [0.0, 1.0]], [[0.0, 1.0], [1.0, 0.0]], [[1.0, 0.0], [0.0, -1.0]], [[0.0, 1.0], [-1.0, 0.0]]], dtype=np.float32)
step_size = 0.2
epsilon = 1e-06

def operator_pairs(term_kind):
    levels = jnp.arange(4, dtype=jnp.int32)
    onehot = (term_kind[:, :, None] == levels).astype(jnp.float32)
    return jnp.einsum('kjo,oxy->kjxy', onehot, jnp.asarray(operator_table, dtype=jnp.float32))

def extend(environment, basis, operators):
    wide = jnp.einsum('kab,bsm->kasm', environment.astype(jnp.float32), basis.astype(jnp.float32)).astype(jnp.bfloat16)
    mixed = jnp.einsum('kst,katm->kasm', operators.astype(jnp.float32), wide.astype(jnp.float32)).astype(jnp.bfloat16)
    return jnp.einsum('asm,kasn->kmn', basis.astype(jnp.float32), mixed.astype(jnp.float32)).astype(jnp.bfloat16)

def extend_twice(environment, first_basis, second_basis, operators):
    return extend(extend(environment, first_basis, operators), second_basis, operators)

def apply_terms(vector, left_env, right_env, operators):
    pair_ops = jnp.einsum('ksx,kty->kstxy', operators[:, 0], operators[:, 1]).reshape(operators.shape[0], 4, 4)
    permuted = jnp.einsum('kxy,ayc->kaxc', pair_ops, vector.astype(jnp.float32)).astype(jnp.bfloat16)
    left_applied = jnp.einsum('kab,kbxc->kaxc', left_env.astype(jnp.float32), permuted.astype(jnp.float32)).astype(jnp.bfloat16)
    groups = N_TERM
    per_group = TERMS // N_TERM
    bond_dim = vector.shape[0]
    grouped = jnp.einsum('gkaxc,gkdc->gaxd', left_applied.astype(jnp.float32).reshape(groups, per_group, bond_dim, 4, bond_dim), right_env.astype(jnp.float32).reshape(groups, per_group, bond_dim, bond_dim))
    rounded = lax.optimization_barrier(grouped.astype(jnp.bfloat16))
    return lax.optimization_barrier(jnp.sum(rounded.astype(jnp.float32), axis=0))

def reference(meet_env, meet_iso, last_site, first_site, term_kind):
    operators = operator_pairs(term_kind)
    sections = meet_env.shape[0]
    bond_dim = meet_env.shape[2]

    def fresh_for(section):
        odd_section = section % 2 == 1
        partner = jnp.bitwise_xor(section, 1).astype(jnp.int32)
        partner_iso = meet_iso[partner]
        own_iso = meet_iso[section]
        first_basis = jnp.where(odd_section, partner_iso, jnp.transpose(partner_iso, (2, 1, 0)))
        second_basis = jnp.where(odd_section, own_iso, jnp.transpose(own_iso, (2, 1, 0)))
        chain_ops = jnp.where(odd_section, operators[:, 0], operators[:, 1])
        return extend_twice(meet_env[partner], first_basis, second_basis, chain_ops)
    fresh_env = lax.map(fresh_for, jnp.arange(sections, dtype=jnp.int32))

    def solve_for(section):
        odd_section = section % 2 == 1
        before = ((section + sections - 1) % sections).astype(jnp.int32)
        left_env = jnp.where(odd_section, meet_env[before], fresh_env[before])
        right_env = jnp.where(odd_section, meet_env[section], fresh_env[section])
        two_site = jnp.dot(last_site[before].reshape(2 * bond_dim, bond_dim), first_site[section].reshape(bond_dim, 2 * bond_dim), preferred_element_type=jnp.float32).reshape(bond_dim, 4, bond_dim)
        for step_index in range(STEPS):
            update = apply_terms(two_site.astype(jnp.bfloat16), left_env, right_env, operators)
            two_site = two_site - step_size * update
        norm_scale = lax.rsqrt(jnp.mean(two_site * two_site) + epsilon)
        return (two_site * norm_scale).reshape(bond_dim, PHYS, PHYS, bond_dim)
    return lax.map(solve_for, jnp.arange(sections, dtype=jnp.int32))
```

```python
import functools

import jax
import jax.numpy as jnp
from jax import lax
from jax.experimental import pallas as pl
from jax.experimental.pallas import tpu as pltpu
from jax.sharding import PartitionSpec as P

STEP = 0.2
EPS = 1e-06
F32 = jnp.float32
BF16 = jnp.bfloat16

VMEM = pl.BlockSpec(memory_space=pltpu.VMEM)
SMEM = pl.BlockSpec(memory_space=pltpu.SMEM)


def nn(a, b):
    return lax.dot_general(a, b, (((1,), (0,)), ((), ())), preferred_element_type=F32)


def nt(a, b):
    return lax.dot_general(a, b, (((1,), (1,)), ((), ())), preferred_element_type=F32)


def identity(n):
    rows = lax.broadcasted_iota(jnp.int32, (n, n), 0)
    cols = lax.broadcasted_iota(jnp.int32, (n, n), 1)
    return (rows == cols).astype(F32).astype(BF16)


def call(body, out_shape, specs, scratch=(), flops=0, nbytes=0, aliases=None, mib=20):
    outs = out_shape if isinstance(out_shape, (tuple, list)) else (out_shape,)
    out_specs = [VMEM] * len(outs)
    return pl.pallas_call(
        body,
        out_shape=list(outs),
        in_specs=list(specs),
        out_specs=out_specs,
        scratch_shapes=list(scratch),
        input_output_aliases=aliases or {},
        compiler_params=pltpu.CompilerParams(vmem_limit_bytes=mib * 2**20),
        cost_estimate=pl.CostEstimate(flops=flops, bytes_accessed=nbytes, transcendentals=0),
    )


def extend(plain, kinds, env, iso, wide, out):
    terms, bond, _ = env.shape
    levels = [iso[s] for s in range(2)]
    if plain:
        eye = identity(bond)
        back = jnp.concatenate([nt(eye, level).astype(BF16) for level in levels], axis=1)
    else:
        back = jnp.concatenate(levels, axis=1)
    for k in range(terms):
        kind = kinds[0 if plain else 1, k]
        crossed = lax.rem(kind, 2) == 1
        lower = jnp.where(kind >= 2, -1.0, 1.0).astype(F32)
        value = env[k]
        left, right = [nn(value, level) if plain else nt(value, level) for level in levels]
        wide[k, :bond] = jnp.where(crossed, right, left).astype(BF16)
        wide[k, bond:] = (jnp.where(crossed, left, right) * lower).astype(BF16)
    for k in range(terms):
        out[k] = nn(back, wide[k]).astype(BF16)


def extend_first_body(place, kinds, env, iso, out, wide):
    for odd in range(2):

        @pl.when(place[0] == odd)
        def _():
            extend(odd == 0, kinds, env, iso, wide, out)


def extend_odd_body(place, kinds, env, iso, out, wide):
    @pl.when(place[0] == 1)
    def _():
        extend(True, kinds, env, iso, wide, out)


def extend_call(body, place, kinds, env, iso):
    terms, bond, _ = env.shape
    return call(
        body,
        jax.ShapeDtypeStruct(env.shape, BF16),
        [SMEM, SMEM, VMEM, VMEM],
        [pltpu.VMEM((terms, 2 * bond, bond), BF16)],
        flops=terms * 8 * bond**3,
        nbytes=4 * terms * bond * bond + 4 * bond * bond,
    )(place, kinds, env, iso)[0]


def store_right(kinds, k, vector, right, applied):
    bond = right.shape[0]
    kind0, kind1 = kinds[0, k], kinds[1, k]
    mask = 2 * lax.rem(kind0, 2) + lax.rem(kind1, 2)
    lower0 = jnp.where(kind0 >= 2, -1.0, 1.0).astype(F32)
    lower1 = jnp.where(kind1 >= 2, -1.0, 1.0).astype(F32)
    for y in range(4):
        part = nt(vector[y], right)
        x = y ^ mask
        sign = jnp.where(x >= 2, lower0, 1.0) * jnp.where(lax.rem(x, 2) == 1, lower1, 1.0)
        applied[x, k * bond : (k + 1) * bond, :] = (part * sign).astype(BF16)


def store_left(lefts, applied, out):
    size, _, rows, _ = out.shape
    joined = jnp.concatenate(lefts, axis=1)
    for x in range(4):
        part = nn(joined, applied[x]).astype(BF16)
        for q in range(size):
            out[q, x] = part[q * rows : (q + 1) * rows]


def first_body(place, kinds, last, first, own_env, partner_env, once, iso, *rest):
    applied, share, out, right_env, exact, vector, wide = rest
    terms, bond, _ = own_env.shape
    rows = share.shape[1]
    for s in range(2):
        before = jnp.where(place[0] == 1, partner_env[terms + s], last[s])
        for t in range(2):
            value = nn(before, first[t])
            exact[2 * s + t] = value
            vector[2 * s + t] = value.astype(BF16)
    start = pl.multiple_of(place[1] * rows, rows)
    for x in range(4):
        share[x] = exact[x, pl.ds(start, rows), :]

    @pl.when(place[0] == 1)
    def _():
        for k in range(terms):
            right = own_env[k]
            right_env[k] = right
            store_right(kinds, k, vector, right, applied)
        store_left([partner_env[k] for k in range(terms)], applied, out)

    @pl.when(place[0] == 0)
    def _():
        extend(False, kinds, once, iso, wide, right_env)
        for k in range(terms):
            store_right(kinds, k, vector, right_env[k], applied)


def first_call(size, place, kinds, last, first, own_env, partner_env, once, iso):
    terms, bond, _ = own_env.shape
    rows = bond // size
    return call(
        first_body,
        [
            jax.ShapeDtypeStruct((4, terms * bond, bond), BF16),
            jax.ShapeDtypeStruct((4, rows, bond), F32),
            jax.ShapeDtypeStruct((size, 4, rows, bond), BF16),
            jax.ShapeDtypeStruct(own_env.shape, BF16),
        ],
        [SMEM, SMEM] + [VMEM] * 6,
        [
            pltpu.VMEM((4, bond, bond), F32),
            pltpu.VMEM((4, bond, bond), BF16),
            pltpu.VMEM((terms, 2 * bond, bond), BF16),
        ],
        flops=(8 + 8 * terms) * bond**3,
        nbytes=(6 * terms + 8 * terms + 16) * bond * bond,
    )(place, kinds, last, first, own_env, partner_env, once, iso)


def second_body(count, place, applied, before, partner_env, *rest):
    pieces, relayed = rest[:count], rest[count:-2]
    out, left_env = rest[-2:]
    terms, bond, _ = left_env.shape

    @pl.when(place[0] == 0)
    def _():
        at = 0
        for n, piece in enumerate(pieces):
            rows = piece.shape[1]
            for k in range(terms):
                value = piece[k]
                if n > 0:
                    value = jnp.where(place[2] == 1, relayed[n - 1][k], value)
                left_env[k, at : at + rows, :] = value
            at += rows
        store_left([left_env[k] for k in range(terms)], applied, out)

    @pl.when(place[0] == 1)
    def _():
        for k in range(terms):
            left_env[k] = partner_env[k]
        for q in range(out.shape[0]):
            out[q] = before[q]


def second_call(place, applied, before, partner_env, pieces, relayed):
    terms, bond, _ = pieces[0].shape[0], before.shape[3], None
    return call(
        functools.partial(second_body, len(pieces)),
        [
            jax.ShapeDtypeStruct(before.shape, BF16),
            jax.ShapeDtypeStruct((terms, bond, bond), BF16),
        ],
        [SMEM] + [VMEM] * (3 + len(pieces) + len(relayed)),
        flops=8 * terms * bond**3,
        nbytes=12 * terms * bond * bond,
    )(place, applied, before, partner_env, *pieces, *relayed)


def apply_body(place, kinds, gathered, left_env, right_env, out, vector, applied):
    size, _, rows, bond = gathered.shape
    terms = left_env.shape[0]
    for q in range(size):
        for x in range(4):
            vector[x, q * rows : (q + 1) * rows, :] = gathered[q, x]
    for k in range(terms):
        store_right(kinds, k, vector, right_env[k], applied)
    store_left([left_env[k] for k in range(terms)], applied, out)


def apply_call(place, kinds, gathered, left_env, right_env):
    terms, bond, _ = left_env.shape
    return call(
        apply_body,
        jax.ShapeDtypeStruct(gathered.shape, BF16),
        [SMEM, SMEM] + [VMEM] * 3,
        [pltpu.VMEM((4, bond, bond), BF16), pltpu.VMEM((4, terms * bond, bond), BF16)],
        flops=16 * terms * bond**3,
        nbytes=8 * terms * bond * bond,
    )(place, kinds, gathered, left_env, right_env)[0]


def update_body(parts, share, new_share, rounded):
    size = parts.shape[0]
    for x in range(4):
        total = parts[0, x].astype(F32)
        for q in range(1, size):
            total = total + parts[q, x].astype(F32)
        value = share[x] - STEP * total
        new_share[x] = value
        rounded[x] = value.astype(BF16)


def update_call(parts, share):
    return call(
        update_body,
        [jax.ShapeDtypeStruct(share.shape, F32), jax.ShapeDtypeStruct(share.shape, BF16)],
        [VMEM, VMEM],
        flops=0,
        nbytes=4 * share.size * 4,
    )(parts, share)


def final_body(gathered, out):
    size, _, rows, bond = gathered.shape
    total = jnp.zeros((rows, bond), F32)
    for q in range(size):
        for x in range(4):
            value = gathered[q, x].astype(F32)
            total = total + value * value
    mean = jnp.sum(total) / (size * 4 * rows * bond)
    scale = lax.rsqrt(jnp.full((8, 128), mean + EPS, F32))[0:1, 0:1]
    halves = bond // 128
    pitch = 4 * halves
    for q in range(size):
        for x in range(4):
            value = gathered[q, x].astype(F32) * scale
            s, t = x // 2, x % 2
            for j in range(halves):
                begin = q * rows * pitch + s * 2 * halves + j * 2 + t
                out[pl.ds(begin, rows, stride=pitch), :] = value[:, j * 128 : (j + 1) * 128]


def final_call(gathered):
    size, _, rows, bond = gathered.shape
    halves = bond // 128
    flat = call(
        final_body,
        jax.ShapeDtypeStruct((size * rows * 4 * halves, 128), F32),
        [VMEM],
        nbytes=gathered.size * 6,
    )(gathered)[0]
    blocks = flat.reshape(size * rows, 2, halves, 2, 128)
    return jnp.transpose(blocks, (0, 1, 3, 2, 4)).reshape(1, size * rows, 2, 2, bond)


def levels_first(site):
    return jnp.transpose(site, (1, 0, 2))


def shards(meet_env, meet_iso, last_site, first_site, term_kind):
    sections, size = lax.axis_size("sec"), lax.axis_size("term")
    both = ("sec", "term")
    own_env = meet_env[0]
    section = lax.axis_index("sec")
    half = sections // 2
    far = (section % half == 0).astype(jnp.int32)
    place = jnp.stack([section % 2, lax.axis_index("term"), far]).astype(jnp.int32)
    kinds = term_kind.T
    bond = own_env.shape[1]

    swap = [(i, i ^ 1) for i in range(sections)]
    to_odd = [(i, i + 1) for i in range(0, sections, 2)]
    to_even = [(i, (i + 1) % sections) for i in range(1, sections, 2)]
    ends = [half - 1, sections - 1]

    def pairs(steps):
        return [(i % sections * size + z, j % sections * size + z) for i, j in steps for z in range(size)]

    near = [(i, j) for i, j in to_even if i not in ends]
    z_first = near + [(i, i + half) for i in ends]
    then_xy = [(i + half, i + 1) for i in ends]

    own_iso = levels_first(meet_iso[0])
    own_last = levels_first(last_site[0])
    once = extend_call(extend_first_body, place, kinds, own_env, own_iso)
    own_last, _ = lax.optimization_barrier((own_last, once))
    once = lax.ppermute(once, "sec", swap)
    came_last = lax.ppermute(own_last, "sec", to_even)
    fresh = extend_call(extend_odd_body, place, kinds, once, own_iso)
    bundle, fresh = lax.optimization_barrier((jnp.concatenate([own_env, own_last]), fresh))
    cut = bond * 5 // 8
    z_piece = lax.ppermute(fresh[:, cut:], both, pairs(z_first))
    direct = lax.ppermute(fresh[:, :cut], both, pairs(to_even))
    partner_env = lax.ppermute(bundle, "sec", to_odd)
    z_piece, came_last = lax.optimization_barrier((z_piece, came_last))
    relayed = lax.ppermute(z_piece, both, pairs(then_xy))
    first = levels_first(first_site[0])
    applied, share, summand, right_env = first_call(
        size, place, kinds, came_last, first, own_env, partner_env, once, own_iso
    )
    summand, left_env = second_call(
        place, applied, summand, partner_env, [direct, z_piece], [relayed]
    )
    parts = lax.all_to_all(summand, "term", 0, 0, tiled=True)
    share, rounded = update_call(parts, share)
    gathered = lax.all_gather(rounded, "term")
    summand = apply_call(place, kinds, gathered, left_env, right_env)
    parts = lax.all_to_all(summand, "term", 0, 0, tiled=True)
    share, rounded = update_call(parts, share)
    gathered = lax.all_gather(rounded, "term")
    return final_call(gathered)


def solution(mesh):
    in_specs = (
        P("sec", "term", None, None),
        P("sec", None, None, None),
        P("sec", None, None, None),
        P("sec", None, None, None),
        P("term", None),
    )
    out_specs = P("sec", None, None, None, None)
    return jax.shard_map(shards, mesh=mesh, in_specs=in_specs, out_specs=out_specs, check_vma=False)
```

```python
import functools

import jax
import jax.numpy as jnp
from jax import lax
from jax.experimental import pallas as pl
from jax.experimental.pallas import tpu as pltpu
from jax.sharding import PartitionSpec as P

STEP = 0.2
EPS = 1e-06
F32 = jnp.float32
BF16 = jnp.bfloat16

VMEM = pl.BlockSpec(memory_space=pltpu.VMEM)
SMEM = pl.BlockSpec(memory_space=pltpu.SMEM)


def nn(a, b):
    return lax.dot_general(a, b, (((1,), (0,)), ((), ())), preferred_element_type=F32)


def nt(a, b):
    return lax.dot_general(a, b, (((1,), (1,)), ((), ())), preferred_element_type=F32)


def identity(n):
    rows = lax.broadcasted_iota(jnp.int32, (n, n), 0)
    cols = lax.broadcasted_iota(jnp.int32, (n, n), 1)
    return (rows == cols).astype(F32).astype(BF16)


def call(body, out_shape, specs, scratch=(), flops=0, nbytes=0, aliases=None, mib=20):
    outs = out_shape if isinstance(out_shape, (tuple, list)) else (out_shape,)
    out_specs = [VMEM] * len(outs)
    return pl.pallas_call(
        body,
        out_shape=list(outs),
        in_specs=list(specs),
        out_specs=out_specs,
        scratch_shapes=list(scratch),
        input_output_aliases=aliases or {},
        compiler_params=pltpu.CompilerParams(vmem_limit_bytes=mib * 2**20),
        cost_estimate=pl.CostEstimate(flops=flops, bytes_accessed=nbytes, transcendentals=0),
    )


def extend(plain, kinds, env, iso, wide, out):
    terms, bond, _ = env.shape
    levels = [iso[s] for s in range(2)]
    if plain:
        eye = identity(bond)
        back = jnp.concatenate([nt(eye, level).astype(BF16) for level in levels], axis=1)
    else:
        back = jnp.concatenate(levels, axis=1)
    for k in range(terms):
        kind = kinds[0 if plain else 1, k]
        crossed = lax.rem(kind, 2) == 1
        lower = jnp.where(kind >= 2, -1.0, 1.0).astype(F32)
        value = env[k]
        left, right = [nn(value, level) if plain else nt(value, level) for level in levels]
        wide[k, :bond] = jnp.where(crossed, right, left).astype(BF16)
        wide[k, bond:] = (jnp.where(crossed, left, right) * lower).astype(BF16)
    for k in range(terms):
        out[k] = nn(back, wide[k]).astype(BF16)


def extend_first_body(place, kinds, env, iso, out, wide):
    for odd in range(2):

        @pl.when(place[0] == odd)
        def _():
            extend(odd == 0, kinds, env, iso, wide, out)


def extend_odd_body(place, kinds, env, iso, out, wide):
    @pl.when(place[0] == 1)
    def _():
        extend(True, kinds, env, iso, wide, out)


def extend_call(body, place, kinds, env, iso):
    terms, bond, _ = env.shape
    return call(
        body,
        jax.ShapeDtypeStruct(env.shape, BF16),
        [SMEM, SMEM, VMEM, VMEM],
        [pltpu.VMEM((terms, 2 * bond, bond), BF16)],
        flops=terms * 8 * bond**3,
        nbytes=4 * terms * bond * bond + 4 * bond * bond,
    )(place, kinds, env, iso)[0]


def store_right(kinds, k, vector, right, applied):
    bond = right.shape[0]
    kind0, kind1 = kinds[0, k], kinds[1, k]
    mask = 2 * lax.rem(kind0, 2) + lax.rem(kind1, 2)
    lower0 = jnp.where(kind0 >= 2, -1.0, 1.0).astype(F32)
    lower1 = jnp.where(kind1 >= 2, -1.0, 1.0).astype(F32)
    for y in range(4):
        part = nt(vector[y], right)
        x = y ^ mask
        sign = jnp.where(x >= 2, lower0, 1.0) * jnp.where(lax.rem(x, 2) == 1, lower1, 1.0)
        applied[x, k * bond : (k + 1) * bond, :] = (part * sign).astype(BF16)


def store_left(lefts, applied, out):
    size, _, rows, _ = out.shape
    joined = jnp.concatenate(lefts, axis=1)
    for x in range(4):
        part = nn(joined, applied[x]).astype(BF16)
        for q in range(size):
            out[q, x] = part[q * rows : (q + 1) * rows]


def first_body(place, kinds, last, first, own_env, partner_env, once, iso, *rest):
    applied, share, out, right_env, exact, vector, wide = rest
    terms, bond, _ = own_env.shape
    rows = share.shape[1]
    for s in range(2):
        before = jnp.where(place[0] == 1, partner_env[terms + s], last[s])
        for t in range(2):
            value = nn(before, first[t])
            exact[2 * s + t] = value
            vector[2 * s + t] = value.astype(BF16)
    start = pl.multiple_of(place[1] * rows, rows)
    for x in range(4):
        share[x] = exact[x, pl.ds(start, rows), :]

    @pl.when(place[0] == 1)
    def _():
        for k in range(terms):
            right = own_env[k]
            right_env[k] = right
            store_right(kinds, k, vector, right, applied)
        store_left([partner_env[k] for k in range(terms)], applied, out)

    @pl.when(place[0] == 0)
    def _():
        extend(False, kinds, once, iso, wide, right_env)
        for k in range(terms):
            store_right(kinds, k, vector, right_env[k], applied)


def first_call(size, place, kinds, last, first, own_env, partner_env, once, iso):
    terms, bond, _ = own_env.shape
    rows = bond // size
    return call(
        first_body,
        [
            jax.ShapeDtypeStruct((4, terms * bond, bond), BF16),
            jax.ShapeDtypeStruct((4, rows, bond), F32),
            jax.ShapeDtypeStruct((size, 4, rows, bond), BF16),
            jax.ShapeDtypeStruct(own_env.shape, BF16),
        ],
        [SMEM, SMEM] + [VMEM] * 6,
        [
            pltpu.VMEM((4, bond, bond), F32),
            pltpu.VMEM((4, bond, bond), BF16),
            pltpu.VMEM((terms, 2 * bond, bond), BF16),
        ],
        flops=(8 + 8 * terms) * bond**3,
        nbytes=(6 * terms + 8 * terms + 16) * bond * bond,
    )(place, kinds, last, first, own_env, partner_env, once, iso)


def second_body(count, place, applied, before, partner_env, *rest):
    pieces, relayed = rest[:count], rest[count:-2]
    out, left_env = rest[-2:]
    terms, bond, _ = left_env.shape

    @pl.when(place[0] == 0)
    def _():
        at = 0
        for n, piece in enumerate(pieces):
            rows = piece.shape[1]
            for k in range(terms):
                value = piece[k]
                if n > 0:
                    value = jnp.where(place[2] == 1, relayed[n - 1][k], value)
                left_env[k, at : at + rows, :] = value
            at += rows
        store_left([left_env[k] for k in range(terms)], applied, out)

    @pl.when(place[0] == 1)
    def _():
        for k in range(terms):
            left_env[k] = partner_env[k]
        for q in range(out.shape[0]):
            out[q] = before[q]


def second_call(place, applied, before, partner_env, pieces, relayed):
    terms, bond, _ = pieces[0].shape[0], before.shape[3], None
    return call(
        functools.partial(second_body, len(pieces)),
        [
            jax.ShapeDtypeStruct(before.shape, BF16),
            jax.ShapeDtypeStruct((terms, bond, bond), BF16),
        ],
        [SMEM] + [VMEM] * (3 + len(pieces) + len(relayed)),
        flops=8 * terms * bond**3,
        nbytes=12 * terms * bond * bond,
    )(place, applied, before, partner_env, *pieces, *relayed)


def apply_body(place, kinds, gathered, left_env, right_env, out, vector, applied):
    size, _, rows, bond = gathered.shape
    terms = left_env.shape[0]
    for q in range(size):
        for x in range(4):
            vector[x, q * rows : (q + 1) * rows, :] = gathered[q, x]
    for k in range(terms):
        store_right(kinds, k, vector, right_env[k], applied)
    store_left([left_env[k] for k in range(terms)], applied, out)


def apply_call(place, kinds, gathered, left_env, right_env):
    terms, bond, _ = left_env.shape
    return call(
        apply_body,
        jax.ShapeDtypeStruct(gathered.shape, BF16),
        [SMEM, SMEM] + [VMEM] * 3,
        [pltpu.VMEM((4, bond, bond), BF16), pltpu.VMEM((4, terms * bond, bond), BF16)],
        flops=16 * terms * bond**3,
        nbytes=8 * terms * bond * bond,
    )(place, kinds, gathered, left_env, right_env)[0]


def update(parts, share):
    share = share - STEP * jnp.sum(parts.astype(F32), axis=0)
    return share, share.astype(BF16)


def final_body(gathered, out):
    size, _, rows, bond = gathered.shape
    total = jnp.zeros((rows, bond), F32)
    for q in range(size):
        for x in range(4):
            value = gathered[q, x].astype(F32)
            total = total + value * value
    mean = jnp.sum(total) / (size * 4 * rows * bond)
    scale = lax.rsqrt(jnp.full((8, 128), mean + EPS, F32))[0:1, 0:1]
    halves = bond // 128
    pitch = 4 * halves
    for q in range(size):
        for x in range(4):
            value = gathered[q, x].astype(F32) * scale
            s, t = x // 2, x % 2
            for j in range(halves):
                begin = q * rows * pitch + s * 2 * halves + j * 2 + t
                out[pl.ds(begin, rows, stride=pitch), :] = value[:, j * 128 : (j + 1) * 128]


def final_call(gathered):
    size, _, rows, bond = gathered.shape
    halves = bond // 128
    flat = call(
        final_body,
        jax.ShapeDtypeStruct((size * rows * 4 * halves, 128), F32),
        [VMEM],
        nbytes=gathered.size * 6,
    )(gathered)[0]
    blocks = flat.reshape(size * rows, 2, halves, 2, 128)
    return jnp.transpose(blocks, (0, 1, 3, 2, 4)).reshape(1, size * rows, 2, 2, bond)


def levels_first(site):
    return jnp.transpose(site, (1, 0, 2))


def shards(meet_env, meet_iso, last_site, first_site, term_kind):
    sections, size = lax.axis_size("sec"), lax.axis_size("term")
    both = ("sec", "term")
    own_env = meet_env[0]
    section = lax.axis_index("sec")
    half = sections // 2
    far = (section % half == 0).astype(jnp.int32)
    place = jnp.stack([section % 2, lax.axis_index("term"), far]).astype(jnp.int32)
    kinds = term_kind.T
    bond = own_env.shape[1]

    swap = [(i, i ^ 1) for i in range(sections)]
    to_odd = [(i, i + 1) for i in range(0, sections, 2)]
    to_even = [(i, (i + 1) % sections) for i in range(1, sections, 2)]
    ends = [half - 1, sections - 1]

    def pairs(steps):
        return [(i % sections * size + z, j % sections * size + z) for i, j in steps for z in range(size)]

    near = [(i, j) for i, j in to_even if i not in ends]
    z_first = near + [(i, i + half) for i in ends]
    then_xy = [(i + half, i + 1) for i in ends]

    own_iso = levels_first(meet_iso[0])
    own_last = levels_first(last_site[0])
    once = extend_call(extend_first_body, place, kinds, own_env, own_iso)
    own_last, _ = lax.optimization_barrier((own_last, once))
    once = lax.ppermute(once, "sec", swap)
    came_last = lax.ppermute(own_last, "sec", to_even)
    fresh = extend_call(extend_odd_body, place, kinds, once, own_iso)
    bundle, fresh = lax.optimization_barrier((jnp.concatenate([own_env, own_last]), fresh))
    cut = bond * 5 // 8
    z_piece = lax.ppermute(fresh[:, cut:], both, pairs(z_first))
    direct = lax.ppermute(fresh[:, :cut], both, pairs(to_even))
    partner_env = lax.ppermute(bundle, "sec", to_odd)
    z_piece, came_last = lax.optimization_barrier((z_piece, came_last))
    relayed = lax.ppermute(z_piece, both, pairs(then_xy))
    first = levels_first(first_site[0])
    applied, share, summand, right_env = first_call(
        size, place, kinds, came_last, first, own_env, partner_env, once, own_iso
    )
    summand, left_env = second_call(
        place, applied, summand, partner_env, [direct, z_piece], [relayed]
    )
    parts = lax.all_to_all(summand, "term", 0, 0, tiled=True)
    share, rounded = update(parts, share)
    gathered = lax.all_gather(rounded, "term")
    summand = apply_call(place, kinds, gathered, left_env, right_env)
    parts = lax.all_to_all(summand, "term", 0, 0, tiled=True)
    share, rounded = update(parts, share)
    gathered = lax.all_gather(rounded, "term")
    return final_call(gathered)


def solution(mesh):
    in_specs = (
        P("sec", "term", None, None),
        P("sec", None, None, None),
        P("sec", None, None, None),
        P("sec", None, None, None),
        P("term", None),
    )
    out_specs = P("sec", None, None, None, None)
    return jax.shard_map(shards, mesh=mesh, in_specs=in_specs, out_specs=out_specs, check_vma=False)
```

```python
import functools

import jax
import jax.numpy as jnp
from jax import lax
from jax.experimental import pallas as pl
from jax.experimental.pallas import tpu as pltpu
from jax.sharding import PartitionSpec as P

STEP = 0.2
EPS = 1e-06
F32 = jnp.float32
BF16 = jnp.bfloat16

FIXED = 3
ROW = 16
CUT = 10

VMEM = pl.BlockSpec(memory_space=pltpu.VMEM)
SMEM = pl.BlockSpec(memory_space=pltpu.SMEM)


def nn(a, b):
    return lax.dot_general(a, b, (((1,), (0,)), ((), ())), preferred_element_type=F32)


def nt(a, b):
    return lax.dot_general(a, b, (((1,), (1,)), ((), ())), preferred_element_type=F32)


def identity(n):
    rows = lax.broadcasted_iota(jnp.int32, (n, n), 0)
    cols = lax.broadcasted_iota(jnp.int32, (n, n), 1)
    return (rows == cols).astype(F32).astype(BF16)


def call(body, out_shape, specs, scratch=(), flops=0, nbytes=0, aliases=None, mib=20):
    outs = out_shape if isinstance(out_shape, (tuple, list)) else (out_shape,)
    out_specs = [VMEM] * len(outs)
    return pl.pallas_call(
        body,
        out_shape=list(outs),
        in_specs=list(specs),
        out_specs=out_specs,
        scratch_shapes=list(scratch),
        input_output_aliases=aliases or {},
        compiler_params=pltpu.CompilerParams(vmem_limit_bytes=mib * 2**20),
        cost_estimate=pl.CostEstimate(flops=flops, bytes_accessed=nbytes, transcendentals=0),
    )


def extend(plain, facts, env, iso, wide, out):
    terms, bond, _ = env.shape
    levels = [iso[s] for s in range(2)]
    if plain:
        eye = identity(bond)
        back = jnp.concatenate([nt(eye, level).astype(BF16) for level in levels], axis=1)
    else:
        back = jnp.concatenate(levels, axis=1)
    for k in range(terms):
        kind = facts[FIXED + (0 if plain else terms) + k]
        crossed = lax.rem(kind, 2) == 1
        lower = jnp.where(kind >= 2, -1.0, 1.0).astype(F32)
        value = env[k]
        left, right = [nn(value, level) if plain else nt(value, level) for level in levels]
        wide[k, :bond] = jnp.where(crossed, right, left).astype(BF16)
        wide[k, bond:] = (jnp.where(crossed, left, right) * lower).astype(BF16)
    for k in range(terms):
        out[k] = nn(back, wide[k]).astype(BF16)


def extend_first_body(facts, env, iso, out, wide):
    for odd in range(2):

        @pl.when(facts[0] == odd)
        def _():
            extend(odd == 0, facts, env, iso, wide, out)


def extend_odd_body(facts, env, iso, out, wide):
    @pl.when(facts[0] == 1)
    def _():
        extend(True, facts, env, iso, wide, out)


def extend_call(body, facts, env, iso):
    terms, bond, _ = env.shape
    return call(
        body,
        jax.ShapeDtypeStruct(env.shape, BF16),
        [SMEM, VMEM, VMEM],
        [pltpu.VMEM((terms, 2 * bond, bond), BF16)],
        flops=terms * 8 * bond**3,
        nbytes=4 * terms * bond * bond + 4 * bond * bond,
    )(facts, env, iso)[0]


def store_right(facts, terms, k, vector, right, applied):
    bond = right.shape[0]
    kind0, kind1 = facts[FIXED + k], facts[FIXED + terms + k]
    mask = 2 * lax.rem(kind0, 2) + lax.rem(kind1, 2)
    lower0 = jnp.where(kind0 >= 2, -1.0, 1.0).astype(F32)
    lower1 = jnp.where(kind1 >= 2, -1.0, 1.0).astype(F32)
    for y in range(4):
        part = nt(vector[y], right)
        x = y ^ mask
        sign = jnp.where(x >= 2, lower0, 1.0) * jnp.where(lax.rem(x, 2) == 1, lower1, 1.0)
        applied[x, k * bond : (k + 1) * bond, :] = (part * sign).astype(BF16)


def store_left(lefts, applied, out):
    size, _, rows, _ = out.shape
    joined = jnp.concatenate(lefts, axis=1)
    for x in range(4):
        part = nn(joined, applied[x]).astype(BF16)
        for q in range(size):
            out[q, x] = part[q * rows : (q + 1) * rows]


def first_body(facts, last, first, own_env, partner, once, iso, *rest):
    applied, share, out, right_env, exact, vector, wide = rest
    terms, bond, _ = own_env.shape
    rows = share.shape[1]
    for s in range(2):
        for t in range(2):
            value = nn(last[s], first[t])
            exact[2 * s + t] = value
            vector[2 * s + t] = value.astype(BF16)
    start = pl.multiple_of(facts[1] * rows, rows)
    for x in range(4):
        share[x] = exact[x, pl.ds(start, rows), :]

    @pl.when(facts[0] == 1)
    def _():
        for k in range(terms):
            right = own_env[k]
            right_env[k] = right
            store_right(facts, terms, k, vector, right, applied)
        store_left([partner[k] for k in range(terms)], applied, out)

    @pl.when(facts[0] == 0)
    def _():
        extend(False, facts, once, iso, wide, right_env)
        for k in range(terms):
            store_right(facts, terms, k, vector, right_env[k], applied)


def first_call(size, facts, last, first, own_env, partner, once, iso):
    terms, bond, _ = own_env.shape
    rows = bond // size
    return call(
        first_body,
        [
            jax.ShapeDtypeStruct((4, terms * bond, bond), BF16),
            jax.ShapeDtypeStruct((4, rows, bond), F32),
            jax.ShapeDtypeStruct((size, 4, rows, bond), BF16),
            jax.ShapeDtypeStruct(own_env.shape, BF16),
        ],
        [SMEM] + [VMEM] * 6,
        [
            pltpu.VMEM((4, bond, bond), F32),
            pltpu.VMEM((4, bond, bond), BF16),
            pltpu.VMEM((terms, 2 * bond, bond), BF16),
        ],
        flops=4000 * bond**3,
    )(facts, last, first, own_env, partner, once, iso)


def second_body(facts, applied, before, partner, came, piece, relayed, out, left_env):
    terms = left_env.shape[0]
    cut = came.shape[1]

    @pl.when(facts[0] == 0)
    def _():
        for k in range(terms):
            left_env[k, :cut] = came[k]
            left_env[k, cut:] = jnp.where(facts[2] == 1, relayed[k], piece[k])
        store_left([left_env[k] for k in range(terms)], applied, out)

    @pl.when(facts[0] == 1)
    def _():
        for k in range(terms):
            left_env[k] = partner[k]
        for q in range(out.shape[0]):
            out[q] = before[q]


def second_call(facts, applied, before, partner, came, piece, relayed):
    terms, _, bond = came.shape
    return call(
        second_body,
        [
            jax.ShapeDtypeStruct(before.shape, BF16),
            jax.ShapeDtypeStruct((terms, bond, bond), BF16),
        ],
        [SMEM] + [VMEM] * 6,
        flops=8 * terms * bond**3,
        nbytes=14 * terms * bond * bond,
    )(facts, applied, before, partner, came, piece, relayed)


def apply_body(facts, gathered, left_env, right_env, out, vector, applied):
    size, _, rows, bond = gathered.shape
    terms = left_env.shape[0]
    for q in range(size):
        for x in range(4):
            vector[x, q * rows : (q + 1) * rows, :] = gathered[q, x]
    for k in range(terms):
        store_right(facts, terms, k, vector, right_env[k], applied)
    store_left([left_env[k] for k in range(terms)], applied, out)


def apply_call(facts, gathered, left_env, right_env):
    terms, bond, _ = left_env.shape
    return call(
        apply_body,
        jax.ShapeDtypeStruct(gathered.shape, BF16),
        [SMEM] + [VMEM] * 3,
        [pltpu.VMEM((4, bond, bond), BF16), pltpu.VMEM((4, terms * bond, bond), BF16)],
        flops=16 * terms * bond**3,
        nbytes=8 * terms * bond * bond,
    )(facts, gathered, left_env, right_env)[0]


def update(parts, share):
    share = share - STEP * jnp.sum(parts.astype(F32), axis=0)
    return share, share.astype(BF16)


def final_body(gathered, out):
    size, _, rows, bond = gathered.shape
    total = jnp.zeros((rows, bond), F32)
    for q in range(size):
        for x in range(4):
            value = gathered[q, x].astype(F32)
            total = total + value * value
    mean = jnp.sum(total) / (size * 4 * rows * bond)
    scale = lax.rsqrt(jnp.full((8, 128), mean + EPS, F32))[0:1, 0:1]
    halves = bond // 128
    pitch = 4 * halves
    for q in range(size):
        for x in range(4):
            value = gathered[q, x].astype(F32) * scale
            s, t = x // 2, x % 2
            for j in range(halves):
                begin = q * rows * pitch + s * 2 * halves + j * 2 + t
                out[pl.ds(begin, rows, stride=pitch), :] = value[:, j * 128 : (j + 1) * 128]


def final_call(gathered):
    size, _, rows, bond = gathered.shape
    halves = bond // 128
    flat = call(
        final_body,
        jax.ShapeDtypeStruct((size * rows * 4 * halves, 128), F32),
        [VMEM],
        nbytes=gathered.size * 6,
    )(gathered)[0]
    blocks = flat.reshape(size * rows, 2, halves, 2, 128)
    return jnp.transpose(blocks, (0, 1, 3, 2, 4)).reshape(1, size * rows, 2, 2, bond)


def levels_first(site):
    return jnp.transpose(site, (1, 0, 2))


def shards(meet_env, meet_iso, last_site, first_site, term_kind):
    sections, size = lax.axis_size("sec"), lax.axis_size("term")
    own_env = meet_env[0]
    section = lax.axis_index("sec")
    odd = section % 2
    far = (section % (sections // 2) == 0).astype(jnp.int32)
    facts = jnp.stack([odd, lax.axis_index("term"), far])
    facts = jnp.concatenate([facts.astype(jnp.int32), term_kind[:, 0], term_kind[:, 1]])
    bond = own_env.shape[1]

    swap = [(i, i ^ 1) for i in range(sections)]
    to_odd = [(i, i + 1) for i in range(0, sections, 2)]
    onward = [(i, (i + 1) % sections) for i in range(sections)]
    odd_on = [(i, (i + 1) % sections) for i in range(1, sections, 2)]

    half = sections // 2
    row = min(ROW, half)
    ends = [half - 1, sections - 1]
    by_row = [(i, j) for i, j in odd_on if i not in ends] + [(i, i - half + row) for i in ends]
    then_on = [(i - half + row, (i + 1) % sections) for i in ends]

    own_iso = levels_first(meet_iso[0])
    own_last = levels_first(last_site[0])
    once = extend_call(extend_first_body, facts, own_env, own_iso)
    raw_env, once = lax.optimization_barrier((own_env, once))
    once = lax.ppermute(once, "sec", swap)
    partner = lax.ppermute(raw_env, "sec", to_odd)
    last = lax.ppermute(own_last, "sec", onward)
    fresh = extend_call(extend_odd_body, facts, once, own_iso)
    cut = CUT * bond // 16
    came = lax.ppermute(fresh[:, :cut], "sec", odd_on)
    piece = lax.ppermute(fresh[:, cut:], "sec", by_row)
    relayed = lax.ppermute(piece, "sec", then_on)
    first = levels_first(first_site[0])
    applied, share, summand, right_env = first_call(
        size, facts, last, first, own_env, partner, once, own_iso
    )
    summand, left_env = second_call(
        facts, applied, summand, partner, came, piece, relayed
    )
    parts = lax.all_to_all(summand, "term", 0, 0, tiled=True)
    share, rounded = update(parts, share)
    gathered = lax.all_gather(rounded, "term")
    summand = apply_call(facts, gathered, left_env, right_env)
    parts = lax.all_to_all(summand, "term", 0, 0, tiled=True)
    share, rounded = update(parts, share)
    gathered = lax.all_gather(rounded, "term")
    return final_call(gathered)


def solution(mesh):
    in_specs = (
        P("sec", "term", None, None),
        P("sec", None, None, None),
        P("sec", None, None, None),
        P("sec", None, None, None),
        P("term", None),
    )
    out_specs = P("sec", None, None, None, None)
    return jax.shard_map(shards, mesh=mesh, in_specs=in_specs, out_specs=out_specs, check_vma=False)
```

```python
import functools

import jax
import jax.numpy as jnp
from jax import lax
from jax.experimental import pallas as pl
from jax.experimental.pallas import tpu as pltpu
from jax.sharding import PartitionSpec as P

STEP = 0.2
EPS = 1e-06
F32 = jnp.float32
BF16 = jnp.bfloat16

FIXED = 3
ROW = 16
CUT = 10

VMEM = pl.BlockSpec(memory_space=pltpu.VMEM)
SMEM = pl.BlockSpec(memory_space=pltpu.SMEM)


def nn(a, b):
    return lax.dot_general(a, b, (((1,), (0,)), ((), ())), preferred_element_type=F32)


def nt(a, b):
    return lax.dot_general(a, b, (((1,), (1,)), ((), ())), preferred_element_type=F32)


def identity(n):
    rows = lax.broadcasted_iota(jnp.int32, (n, n), 0)
    cols = lax.broadcasted_iota(jnp.int32, (n, n), 1)
    return (rows == cols).astype(F32).astype(BF16)


def call(body, out_shape, specs, scratch=(), flops=0, nbytes=0, aliases=None, mib=20):
    outs = out_shape if isinstance(out_shape, (tuple, list)) else (out_shape,)
    out_specs = [VMEM] * len(outs)
    return pl.pallas_call(
        body,
        out_shape=list(outs),
        in_specs=list(specs),
        out_specs=out_specs,
        scratch_shapes=list(scratch),
        input_output_aliases=aliases or {},
        compiler_params=pltpu.CompilerParams(vmem_limit_bytes=mib * 2**20),
        cost_estimate=pl.CostEstimate(flops=flops, bytes_accessed=nbytes, transcendentals=0),
    )


def extend(plain, facts, env, iso, wide, out):
    terms, bond, _ = env.shape
    levels = [iso[s] for s in range(2)]
    if plain:
        eye = identity(bond)
        back = jnp.concatenate([nt(eye, level).astype(BF16) for level in levels], axis=1)
    else:
        back = jnp.concatenate(levels, axis=1)
    for k in range(terms):
        kind = facts[FIXED + (0 if plain else terms) + k]
        crossed = lax.rem(kind, 2) == 1
        lower = jnp.where(kind >= 2, -1.0, 1.0).astype(F32)
        value = env[k]
        left, right = [nn(value, level) if plain else nt(value, level) for level in levels]
        wide[k, :bond] = jnp.where(crossed, right, left).astype(BF16)
        wide[k, bond:] = (jnp.where(crossed, left, right) * lower).astype(BF16)
    for k in range(terms):
        out[k] = nn(back, wide[k]).astype(BF16)


def extend_first_body(facts, env, iso, out, wide):
    for odd in range(2):

        @pl.when(facts[0] == odd)
        def _():
            extend(odd == 0, facts, env, iso, wide, out)


def extend_odd_body(facts, env, iso, out, wide):
    @pl.when(facts[0] == 1)
    def _():
        extend(True, facts, env, iso, wide, out)


def extend_call(body, facts, env, iso):
    terms, bond, _ = env.shape
    return call(
        body,
        jax.ShapeDtypeStruct(env.shape, BF16),
        [SMEM, VMEM, VMEM],
        [pltpu.VMEM((terms, 2 * bond, bond), BF16)],
        flops=terms * 8 * bond**3,
        nbytes=4 * terms * bond * bond + 4 * bond * bond,
    )(facts, env, iso)[0]


def store_right(facts, terms, k, vector, right, applied):
    bond = right.shape[0]
    kind0, kind1 = facts[FIXED + k], facts[FIXED + terms + k]
    mask = 2 * lax.rem(kind0, 2) + lax.rem(kind1, 2)
    lower0 = jnp.where(kind0 >= 2, -1.0, 1.0).astype(F32)
    lower1 = jnp.where(kind1 >= 2, -1.0, 1.0).astype(F32)
    for y in range(4):
        part = nt(vector[y], right)
        x = y ^ mask
        sign = jnp.where(x >= 2, lower0, 1.0) * jnp.where(lax.rem(x, 2) == 1, lower1, 1.0)
        applied[x, k * bond : (k + 1) * bond, :] = (part * sign).astype(BF16)


def store_left(lefts, applied, out):
    size, _, rows, _ = out.shape
    joined = jnp.concatenate(lefts, axis=1)
    for x in range(4):
        part = nn(joined, applied[x]).astype(BF16)
        for q in range(size):
            out[q, x] = part[q * rows : (q + 1) * rows]


def first_body(facts, last, first, own_env, partner, once, iso, *rest):
    applied, share, out, right_env, exact, vector, wide = rest
    terms, bond, _ = own_env.shape
    rows = share.shape[1]
    for s in range(2):
        for t in range(2):
            value = nn(last[s], first[t])
            exact[2 * s + t] = value
            vector[2 * s + t] = value.astype(BF16)
    start = pl.multiple_of(facts[1] * rows, rows)
    for x in range(4):
        share[x] = exact[x, pl.ds(start, rows), :]

    @pl.when(facts[0] == 1)
    def _():
        for k in range(terms):
            right = own_env[k]
            right_env[k] = right
            store_right(facts, terms, k, vector, right, applied)
        store_left([partner[k] for k in range(terms)], applied, out)

    @pl.when(facts[0] == 0)
    def _():
        extend(False, facts, once, iso, wide, right_env)
        for k in range(terms):
            store_right(facts, terms, k, vector, right_env[k], applied)


def first_call(size, facts, last, first, own_env, partner, once, iso):
    terms, bond, _ = own_env.shape
    rows = bond // size
    return call(
        first_body,
        [
            jax.ShapeDtypeStruct((4, terms * bond, bond), BF16),
            jax.ShapeDtypeStruct((4, rows, bond), F32),
            jax.ShapeDtypeStruct((size, 4, rows, bond), BF16),
            jax.ShapeDtypeStruct(own_env.shape, BF16),
        ],
        [SMEM] + [VMEM] * 6,
        [
            pltpu.VMEM((4, bond, bond), F32),
            pltpu.VMEM((4, bond, bond), BF16),
            pltpu.VMEM((terms, 2 * bond, bond), BF16),
        ],
        flops=4000 * bond**3,
    )(facts, last, first, own_env, partner, once, iso)


def second_body(facts, applied, before, partner, came, piece, relayed, out, left_env):
    terms = left_env.shape[0]
    cut = came.shape[1]

    @pl.when(facts[0] == 0)
    def _():
        for k in range(terms):
            left_env[k, :cut] = came[k]
            left_env[k, cut:] = jnp.where(facts[2] == 1, relayed[k], piece[k])
        store_left([left_env[k] for k in range(terms)], applied, out)

    @pl.when(facts[0] == 1)
    def _():
        for k in range(terms):
            left_env[k] = partner[k]
        for q in range(out.shape[0]):
            out[q] = before[q]


def second_call(facts, applied, before, partner, came, piece, relayed):
    terms, _, bond = came.shape
    return call(
        second_body,
        [
            jax.ShapeDtypeStruct(before.shape, BF16),
            jax.ShapeDtypeStruct((terms, bond, bond), BF16),
        ],
        [SMEM] + [VMEM] * 6,
        flops=8 * terms * bond**3,
        nbytes=14 * terms * bond * bond,
    )(facts, applied, before, partner, came, piece, relayed)


def apply_body(facts, gathered, left_env, right_env, out, vector, applied):
    size, _, rows, bond = gathered.shape
    terms = left_env.shape[0]
    for q in range(size):
        for x in range(4):
            vector[x, q * rows : (q + 1) * rows, :] = gathered[q, x]
    for k in range(terms):
        store_right(facts, terms, k, vector, right_env[k], applied)
    store_left([left_env[k] for k in range(terms)], applied, out)


def apply_call(facts, gathered, left_env, right_env):
    terms, bond, _ = left_env.shape
    return call(
        apply_body,
        jax.ShapeDtypeStruct(gathered.shape, BF16),
        [SMEM] + [VMEM] * 3,
        [pltpu.VMEM((4, bond, bond), BF16), pltpu.VMEM((4, terms * bond, bond), BF16)],
        flops=16 * terms * bond**3,
        nbytes=8 * terms * bond * bond,
    )(facts, gathered, left_env, right_env)[0]


def update(parts, share):
    share = share - STEP * jnp.sum(parts.astype(F32), axis=0)
    return share, share.astype(BF16)


def final_body(gathered, out):
    size, _, rows, bond = gathered.shape
    total = jnp.zeros((rows, bond), F32)
    for q in range(size):
        for x in range(4):
            value = gathered[q, x].astype(F32)
            total = total + value * value
    mean = jnp.sum(total) / (size * 4 * rows * bond)
    scale = lax.rsqrt(jnp.full((8, 128), mean + EPS, F32))[0:1, 0:1]
    halves = bond // 128
    pitch = 4 * halves
    for q in range(size):
        for x in range(4):
            value = gathered[q, x].astype(F32) * scale
            s, t = x // 2, x % 2
            for j in range(halves):
                begin = q * rows * pitch + s * 2 * halves + j * 2 + t
                out[pl.ds(begin, rows, stride=pitch), :] = value[:, j * 128 : (j + 1) * 128]


def final_call(gathered):
    size, _, rows, bond = gathered.shape
    halves = bond // 128
    flat = call(
        final_body,
        jax.ShapeDtypeStruct((size * rows * 4 * halves, 128), F32),
        [VMEM],
        nbytes=gathered.size * 6,
    )(gathered)[0]
    blocks = flat.reshape(size * rows, 2, halves, 2, 128)
    return jnp.transpose(blocks, (0, 1, 3, 2, 4)).reshape(1, size * rows, 2, 2, bond)


def levels_first(site):
    return jnp.transpose(site, (1, 0, 2))


def shards(meet_env, meet_iso, last_site, first_site, term_kind):
    sections, size = lax.axis_size("sec"), lax.axis_size("term")
    own_env = meet_env[0]
    section = lax.axis_index("sec")
    odd = section % 2
    far = (section % (sections // 2) == 0).astype(jnp.int32)
    facts = jnp.stack([odd, lax.axis_index("term"), far])
    facts = jnp.concatenate([facts.astype(jnp.int32), term_kind[:, 0], term_kind[:, 1]])
    bond = own_env.shape[1]

    swap = [(i, i ^ 1) for i in range(sections)]
    to_odd = [(i, i + 1) for i in range(0, sections, 2)]
    onward = [(i, (i + 1) % sections) for i in range(sections)]
    odd_on = [(i, (i + 1) % sections) for i in range(1, sections, 2)]

    half = sections // 2
    row = min(ROW, half)
    ends = [half - 1, sections - 1]
    by_row = [(i, j) for i, j in odd_on if i not in ends] + [(i, i - half + row) for i in ends]
    then_on = [(i - half + row, (i + 1) % sections) for i in ends]

    own_iso = levels_first(meet_iso[0])
    own_last = levels_first(last_site[0])
    once = extend_call(extend_first_body, facts, own_env, own_iso)
    raw_env, once = lax.optimization_barrier((own_env, once))
    once = lax.ppermute(once, "sec", swap)
    partner = lax.ppermute(raw_env, "sec", to_odd)
    last = lax.ppermute(own_last, "sec", onward)
    fresh = extend_call(extend_odd_body, facts, once, own_iso)
    cut = CUT * bond // 16
    came = lax.ppermute(fresh[:, :cut], "sec", odd_on)
    piece = lax.ppermute(fresh[:, cut:], "sec", by_row)
    relayed = lax.ppermute(piece, "sec", then_on)
    first = levels_first(first_site[0])
    applied, share, summand, right_env = first_call(
        size, facts, last, first, own_env, partner, once, own_iso
    )
    summand, left_env = second_call(
        facts, applied, summand, partner, came, piece, relayed
    )
    parts = lax.all_to_all(summand, "term", 0, 0, tiled=True)
    share, rounded = update(parts, share)
    gathered = lax.all_gather(rounded, "term")
    summand = apply_call(facts, gathered, left_env, right_env)
    parts = lax.all_to_all(summand, "term", 0, 0, tiled=True)
    share, rounded = update(parts, share)
    copies = jnp.broadcast_to(rounded, (size, *rounded.shape))
    gathered = lax.all_to_all(copies, "term", 0, 0, tiled=True)
    return final_call(gathered)


def solution(mesh):
    in_specs = (
        P("sec", "term", None, None),
        P("sec", None, None, None),
        P("sec", None, None, None),
        P("sec", None, None, None),
        P("term", None),
    )
    out_specs = P("sec", None, None, None, None)
    return jax.shard_map(shards, mesh=mesh, in_specs=in_specs, out_specs=out_specs, check_vma=False)
```

```python
import functools

import jax
import jax.numpy as jnp
from jax import lax
from jax.experimental import pallas as pl
from jax.experimental.pallas import tpu as pltpu
from jax.sharding import PartitionSpec as P

STEP = 0.2
EPS = 1e-06
F32 = jnp.float32
BF16 = jnp.bfloat16

FIXED = 3
ROW = 16
CUT = 10

VMEM = pl.BlockSpec(memory_space=pltpu.VMEM)
SMEM = pl.BlockSpec(memory_space=pltpu.SMEM)


def nn(a, b):
    return lax.dot_general(a, b, (((1,), (0,)), ((), ())), preferred_element_type=F32)


def nt(a, b):
    return lax.dot_general(a, b, (((1,), (1,)), ((), ())), preferred_element_type=F32)


def identity(n):
    rows = lax.broadcasted_iota(jnp.int32, (n, n), 0)
    cols = lax.broadcasted_iota(jnp.int32, (n, n), 1)
    return (rows == cols).astype(F32).astype(BF16)


def call(body, out_shape, specs, scratch=(), flops=0, nbytes=0, aliases=None, mib=20):
    outs = out_shape if isinstance(out_shape, (tuple, list)) else (out_shape,)
    out_specs = [VMEM] * len(outs)
    return pl.pallas_call(
        body,
        out_shape=list(outs),
        in_specs=list(specs),
        out_specs=out_specs,
        scratch_shapes=list(scratch),
        input_output_aliases=aliases or {},
        compiler_params=pltpu.CompilerParams(vmem_limit_bytes=mib * 2**20),
        cost_estimate=pl.CostEstimate(flops=flops, bytes_accessed=nbytes, transcendentals=0),
    )


def extend(plain, facts, env, iso, wide, out):
    terms, bond, _ = env.shape
    levels = [iso[s] for s in range(2)]
    if plain:
        eye = identity(bond)
        back = jnp.concatenate([nt(eye, level).astype(BF16) for level in levels], axis=1)
    else:
        back = jnp.concatenate(levels, axis=1)
    for k in range(terms):
        kind = facts[FIXED + (0 if plain else terms) + k]
        crossed = lax.rem(kind, 2) == 1
        lower = jnp.where(kind >= 2, -1.0, 1.0).astype(F32)
        value = env[k]
        left, right = [nn(value, level) if plain else nt(value, level) for level in levels]
        wide[k, :bond] = jnp.where(crossed, right, left).astype(BF16)
        wide[k, bond:] = (jnp.where(crossed, left, right) * lower).astype(BF16)
    for k in range(terms):
        out[k] = nn(back, wide[k]).astype(BF16)


def extend_first_body(facts, env, iso, out, wide):
    for odd in range(2):

        @pl.when(facts[0] == odd)
        def _():
            extend(odd == 0, facts, env, iso, wide, out)


def extend_odd_body(facts, env, iso, out, wide):
    @pl.when(facts[0] == 1)
    def _():
        extend(True, facts, env, iso, wide, out)


def extend_call(body, facts, env, iso):
    terms, bond, _ = env.shape
    return call(
        body,
        jax.ShapeDtypeStruct(env.shape, BF16),
        [SMEM, VMEM, VMEM],
        [pltpu.VMEM((terms, 2 * bond, bond), BF16)],
        flops=terms * 8 * bond**3,
        nbytes=4 * terms * bond * bond + 4 * bond * bond,
    )(facts, env, iso)[0]


def store_right(facts, terms, k, vector, right, applied):
    bond = right.shape[0]
    kind0, kind1 = facts[FIXED + k], facts[FIXED + terms + k]
    mask = 2 * lax.rem(kind0, 2) + lax.rem(kind1, 2)
    lower0 = jnp.where(kind0 >= 2, -1.0, 1.0).astype(F32)
    lower1 = jnp.where(kind1 >= 2, -1.0, 1.0).astype(F32)
    for y in range(4):
        part = nt(vector[y], right)
        x = y ^ mask
        sign = jnp.where(x >= 2, lower0, 1.0) * jnp.where(lax.rem(x, 2) == 1, lower1, 1.0)
        applied[x, k * bond : (k + 1) * bond, :] = (part * sign).astype(BF16)


def store_left(lefts, applied, out):
    size, _, rows, _ = out.shape
    joined = jnp.concatenate(lefts, axis=1)
    for x in range(4):
        part = nn(joined, applied[x]).astype(BF16)
        for q in range(size):
            out[q, x] = part[q * rows : (q + 1) * rows]


def first_body(facts, last, first, own_env, partner, once, iso, *rest):
    applied, share, out, right_env, exact, vector, wide = rest
    terms, bond, _ = own_env.shape
    rows = share.shape[1]
    for s in range(2):
        for t in range(2):
            value = nn(last[s], first[t])
            exact[2 * s + t] = value
            vector[2 * s + t] = value.astype(BF16)
    start = pl.multiple_of(facts[1] * rows, rows)
    for x in range(4):
        share[x] = exact[x, pl.ds(start, rows), :]

    @pl.when(facts[0] == 1)
    def _():
        for k in range(terms):
            right = own_env[k]
            right_env[k] = right
            store_right(facts, terms, k, vector, right, applied)
        store_left([partner[k] for k in range(terms)], applied, out)

    @pl.when(facts[0] == 0)
    def _():
        extend(False, facts, once, iso, wide, right_env)
        for k in range(terms):
            store_right(facts, terms, k, vector, right_env[k], applied)


def first_call(size, facts, last, first, own_env, partner, once, iso):
    terms, bond, _ = own_env.shape
    rows = bond // size
    return call(
        first_body,
        [
            jax.ShapeDtypeStruct((4, terms * bond, bond), BF16),
            jax.ShapeDtypeStruct((4, rows, bond), F32),
            jax.ShapeDtypeStruct((size, 4, rows, bond), BF16),
            jax.ShapeDtypeStruct(own_env.shape, BF16),
        ],
        [SMEM] + [VMEM] * 6,
        [
            pltpu.VMEM((4, bond, bond), F32),
            pltpu.VMEM((4, bond, bond), BF16),
            pltpu.VMEM((terms, 2 * bond, bond), BF16),
        ],
        flops=4000 * bond**3,
    )(facts, last, first, own_env, partner, once, iso)


def second_body(facts, applied, before, partner, came, piece, relayed, out, left_env):
    terms = left_env.shape[0]
    cut = came.shape[1]

    @pl.when(facts[0] == 0)
    def _():
        for k in range(terms):
            left_env[k, :cut] = came[k]
            left_env[k, cut:] = jnp.where(facts[2] == 1, relayed[k], piece[k])
        store_left([left_env[k] for k in range(terms)], applied, out)

    @pl.when(facts[0] == 1)
    def _():
        for k in range(terms):
            left_env[k] = partner[k]
        for q in range(out.shape[0]):
            out[q] = before[q]


def second_call(facts, applied, before, partner, came, piece, relayed):
    terms, _, bond = came.shape
    return call(
        second_body,
        [
            jax.ShapeDtypeStruct(before.shape, BF16),
            jax.ShapeDtypeStruct((terms, bond, bond), BF16),
        ],
        [SMEM] + [VMEM] * 6,
        flops=8 * terms * bond**3,
        nbytes=14 * terms * bond * bond,
    )(facts, applied, before, partner, came, piece, relayed)


def apply_body(facts, gathered, left_env, right_env, out, vector, applied):
    size, _, rows, bond = gathered.shape
    terms = left_env.shape[0]
    for q in range(size):
        for x in range(4):
            vector[x, q * rows : (q + 1) * rows, :] = gathered[q, x]
    for k in range(terms):
        store_right(facts, terms, k, vector, right_env[k], applied)
    store_left([left_env[k] for k in range(terms)], applied, out)


def apply_call(facts, gathered, left_env, right_env):
    terms, bond, _ = left_env.shape
    return call(
        apply_body,
        jax.ShapeDtypeStruct(gathered.shape, BF16),
        [SMEM] + [VMEM] * 3,
        [pltpu.VMEM((4, bond, bond), BF16), pltpu.VMEM((4, terms * bond, bond), BF16)],
        flops=16 * terms * bond**3,
        nbytes=8 * terms * bond * bond,
    )(facts, gathered, left_env, right_env)[0]


def update(parts, share):
    share = share - STEP * jnp.sum(parts.astype(F32), axis=0)
    return share, share.astype(BF16)


def final_body(gathered, out):
    size, _, rows, bond = gathered.shape
    total = jnp.zeros((rows, bond), F32)
    for q in range(size):
        for x in range(4):
            value = gathered[q, x].astype(F32)
            total = total + value * value
    mean = jnp.sum(total) / (size * 4 * rows * bond)
    scale = lax.rsqrt(jnp.full((8, 128), mean + EPS, F32))[0:1, 0:1]
    halves = bond // 128
    pitch = 4 * halves
    for q in range(size):
        for x in range(4):
            value = gathered[q, x].astype(F32) * scale
            s, t = x // 2, x % 2
            for j in range(halves):
                begin = q * rows * pitch + s * 2 * halves + j * 2 + t
                out[pl.ds(begin, rows, stride=pitch), :] = value[:, j * 128 : (j + 1) * 128]


def final_call(gathered):
    size, _, rows, bond = gathered.shape
    halves = bond // 128
    flat = call(
        final_body,
        jax.ShapeDtypeStruct((size * rows * 4 * halves, 128), F32),
        [VMEM],
        nbytes=gathered.size * 6,
    )(gathered)[0]
    blocks = flat.reshape(size * rows, 2, halves, 2, 128)
    return jnp.transpose(blocks, (0, 1, 3, 2, 4)).reshape(1, size * rows, 2, 2, bond)


def levels_first(site):
    return jnp.transpose(site, (1, 0, 2))


def shards(meet_env, meet_iso, last_site, first_site, term_kind):
    sections, size = lax.axis_size("sec"), lax.axis_size("term")
    own_env = meet_env[0]
    section = lax.axis_index("sec")
    odd = section % 2
    far = (section % (sections // 2) == 0).astype(jnp.int32)
    facts = jnp.stack([odd, lax.axis_index("term"), far])
    facts = jnp.concatenate([facts.astype(jnp.int32), term_kind[:, 0], term_kind[:, 1]])
    bond = own_env.shape[1]

    swap = [(i, i ^ 1) for i in range(sections)]
    to_odd = [(i, i + 1) for i in range(0, sections, 2)]
    onward = [(i, (i + 1) % sections) for i in range(sections)]
    odd_on = [(i, (i + 1) % sections) for i in range(1, sections, 2)]

    half = sections // 2
    row = min(ROW, half)
    ends = [half - 1, sections - 1]
    by_row = [(i, j) for i, j in odd_on if i not in ends] + [(i, i - half + row) for i in ends]
    then_on = [(i - half + row, (i + 1) % sections) for i in ends]

    own_iso = levels_first(meet_iso[0])
    own_last = levels_first(last_site[0])
    once = extend_call(extend_first_body, facts, own_env, own_iso)
    raw_env, once = lax.optimization_barrier((own_env, once))
    once = lax.ppermute(once, "sec", swap)
    partner = lax.ppermute(raw_env, "sec", to_odd)
    last = lax.ppermute(own_last, "sec", onward)
    fresh = extend_call(extend_odd_body, facts, once, own_iso)
    cut = CUT * bond // 16
    came = lax.ppermute(fresh[:, :cut], "sec", odd_on)
    piece = lax.ppermute(fresh[:, cut:], "sec", by_row)
    relayed = lax.ppermute(piece, "sec", then_on)
    first = levels_first(first_site[0])
    applied, share, summand, right_env = first_call(
        size, facts, last, first, own_env, partner, once, own_iso
    )
    summand, left_env = second_call(
        facts, applied, summand, partner, came, piece, relayed
    )
    parts = lax.all_to_all(summand, "term", 0, 0, tiled=True)
    share, rounded = update(parts, share)
    copies = jnp.broadcast_to(rounded, (size, *rounded.shape))
    gathered = lax.all_to_all(copies, "term", 0, 0, tiled=True)
    summand = apply_call(facts, gathered, left_env, right_env)
    parts = lax.all_to_all(summand, "term", 0, 0, tiled=True)
    share, rounded = update(parts, share)
    copies = jnp.broadcast_to(rounded, (size, *rounded.shape))
    gathered = lax.all_to_all(copies, "term", 0, 0, tiled=True)
    return final_call(gathered)


def solution(mesh):
    in_specs = (
        P("sec", "term", None, None),
        P("sec", None, None, None),
        P("sec", None, None, None),
        P("sec", None, None, None),
        P("term", None),
    )
    out_specs = P("sec", None, None, None, None)
    return jax.shard_map(shards, mesh=mesh, in_specs=in_specs, out_specs=out_specs, check_vma=False)
```

```python
import functools

import jax
import jax.numpy as jnp
from jax import lax
from jax.experimental import pallas as pl
from jax.experimental.pallas import tpu as pltpu
from jax.sharding import PartitionSpec as P

STEP = 0.2
EPS = 1e-06
F32 = jnp.float32
BF16 = jnp.bfloat16

FIXED = 3
ROW = 16
CUT = 9

VMEM = pl.BlockSpec(memory_space=pltpu.VMEM)
SMEM = pl.BlockSpec(memory_space=pltpu.SMEM)


def nn(a, b):
    return lax.dot_general(a, b, (((1,), (0,)), ((), ())), preferred_element_type=F32)


def nt(a, b):
    return lax.dot_general(a, b, (((1,), (1,)), ((), ())), preferred_element_type=F32)


def identity(n):
    rows = lax.broadcasted_iota(jnp.int32, (n, n), 0)
    cols = lax.broadcasted_iota(jnp.int32, (n, n), 1)
    return (rows == cols).astype(F32).astype(BF16)


def call(body, out_shape, specs, scratch=(), flops=0, nbytes=0, aliases=None, mib=20):
    outs = out_shape if isinstance(out_shape, (tuple, list)) else (out_shape,)
    out_specs = [VMEM] * len(outs)
    return pl.pallas_call(
        body,
        out_shape=list(outs),
        in_specs=list(specs),
        out_specs=out_specs,
        scratch_shapes=list(scratch),
        input_output_aliases=aliases or {},
        compiler_params=pltpu.CompilerParams(vmem_limit_bytes=mib * 2**20),
        cost_estimate=pl.CostEstimate(flops=flops, bytes_accessed=nbytes, transcendentals=0),
    )


def extend(plain, facts, env, iso, wide, out):
    terms, bond, _ = env.shape
    levels = [iso[s] for s in range(2)]
    if plain:
        eye = identity(bond)
        back = jnp.concatenate([nt(eye, level).astype(BF16) for level in levels], axis=1)
    else:
        back = jnp.concatenate(levels, axis=1)
    for k in range(terms):
        kind = facts[FIXED + (0 if plain else terms) + k]
        crossed = lax.rem(kind, 2) == 1
        lower = jnp.where(kind >= 2, -1.0, 1.0).astype(F32)
        value = env[k]
        left, right = [nn(value, level) if plain else nt(value, level) for level in levels]
        wide[k, :bond] = jnp.where(crossed, right, left).astype(BF16)
        wide[k, bond:] = (jnp.where(crossed, left, right) * lower).astype(BF16)
    for k in range(terms):
        out[k] = nn(back, wide[k]).astype(BF16)


def extend_first_body(facts, env, iso, out, wide):
    for odd in range(2):

        @pl.when(facts[0] == odd)
        def _():
            extend(odd == 0, facts, env, iso, wide, out)


def extend_odd_body(facts, env, iso, out, wide):
    @pl.when(facts[0] == 1)
    def _():
        extend(True, facts, env, iso, wide, out)


def extend_call(body, facts, env, iso):
    terms, bond, _ = env.shape
    return call(
        body,
        jax.ShapeDtypeStruct(env.shape, BF16),
        [SMEM, VMEM, VMEM],
        [pltpu.VMEM((terms, 2 * bond, bond), BF16)],
        flops=terms * 8 * bond**3,
        nbytes=4 * terms * bond * bond + 4 * bond * bond,
    )(facts, env, iso)[0]


def store_right(facts, terms, k, vector, right, applied):
    bond = right.shape[0]
    kind0, kind1 = facts[FIXED + k], facts[FIXED + terms + k]
    mask = 2 * lax.rem(kind0, 2) + lax.rem(kind1, 2)
    lower0 = jnp.where(kind0 >= 2, -1.0, 1.0).astype(F32)
    lower1 = jnp.where(kind1 >= 2, -1.0, 1.0).astype(F32)
    for y in range(4):
        part = nt(vector[y], right)
        x = y ^ mask
        sign = jnp.where(x >= 2, lower0, 1.0) * jnp.where(lax.rem(x, 2) == 1, lower1, 1.0)
        applied[x, k * bond : (k + 1) * bond, :] = (part * sign).astype(BF16)


def store_left(lefts, applied, out):
    size, _, rows, _ = out.shape
    joined = jnp.concatenate(lefts, axis=1)
    for x in range(4):
        part = nn(joined, applied[x]).astype(BF16)
        for q in range(size):
            out[q, x] = part[q * rows : (q + 1) * rows]


def first_body(facts, last, first, own_env, partner, once, iso, *rest):
    applied, share, out, right_env, exact, vector, wide = rest
    terms, bond, _ = own_env.shape
    rows = share.shape[1]
    for s in range(2):
        for t in range(2):
            value = nn(last[s], first[t])
            exact[2 * s + t] = value
            vector[2 * s + t] = value.astype(BF16)
    start = pl.multiple_of(facts[1] * rows, rows)
    for x in range(4):
        share[x] = exact[x, pl.ds(start, rows), :]

    @pl.when(facts[0] == 1)
    def _():
        for k in range(terms):
            right = own_env[k]
            right_env[k] = right
            store_right(facts, terms, k, vector, right, applied)
        store_left([partner[k] for k in range(terms)], applied, out)

    @pl.when(facts[0] == 0)
    def _():
        extend(False, facts, once, iso, wide, right_env)
        for k in range(terms):
            store_right(facts, terms, k, vector, right_env[k], applied)


def first_call(size, facts, last, first, own_env, partner, once, iso):
    terms, bond, _ = own_env.shape
    rows = bond // size
    return call(
        first_body,
        [
            jax.ShapeDtypeStruct((4, terms * bond, bond), BF16),
            jax.ShapeDtypeStruct((4, rows, bond), F32),
            jax.ShapeDtypeStruct((size, 4, rows, bond), BF16),
            jax.ShapeDtypeStruct(own_env.shape, BF16),
        ],
        [SMEM] + [VMEM] * 6,
        [
            pltpu.VMEM((4, bond, bond), F32),
            pltpu.VMEM((4, bond, bond), BF16),
            pltpu.VMEM((terms, 2 * bond, bond), BF16),
        ],
        flops=4000 * bond**3,
    )(facts, last, first, own_env, partner, once, iso)


def second_body(facts, applied, before, partner, came, piece, relayed, out, left_env):
    terms = left_env.shape[0]
    cut = came.shape[1]

    @pl.when(facts[0] == 0)
    def _():
        for k in range(terms):
            left_env[k, :cut] = came[k]
            left_env[k, cut:] = jnp.where(facts[2] == 1, relayed[k], piece[k])
        store_left([left_env[k] for k in range(terms)], applied, out)

    @pl.when(facts[0] == 1)
    def _():
        for k in range(terms):
            left_env[k] = partner[k]
        for q in range(out.shape[0]):
            out[q] = before[q]


def second_call(facts, applied, before, partner, came, piece, relayed):
    terms, _, bond = came.shape
    return call(
        second_body,
        [
            jax.ShapeDtypeStruct(before.shape, BF16),
            jax.ShapeDtypeStruct((terms, bond, bond), BF16),
        ],
        [SMEM] + [VMEM] * 6,
        flops=8 * terms * bond**3,
        nbytes=14 * terms * bond * bond,
    )(facts, applied, before, partner, came, piece, relayed)


def apply_body(facts, gathered, left_env, right_env, out, vector, applied):
    size, _, rows, bond = gathered.shape
    terms = left_env.shape[0]
    for q in range(size):
        for x in range(4):
            vector[x, q * rows : (q + 1) * rows, :] = gathered[q, x]
    for k in range(terms):
        store_right(facts, terms, k, vector, right_env[k], applied)
    store_left([left_env[k] for k in range(terms)], applied, out)


def apply_call(facts, gathered, left_env, right_env):
    terms, bond, _ = left_env.shape
    return call(
        apply_body,
        jax.ShapeDtypeStruct(gathered.shape, BF16),
        [SMEM] + [VMEM] * 3,
        [pltpu.VMEM((4, bond, bond), BF16), pltpu.VMEM((4, terms * bond, bond), BF16)],
        flops=16 * terms * bond**3,
        nbytes=8 * terms * bond * bond,
    )(facts, gathered, left_env, right_env)[0]


def update(parts, share):
    share = share - STEP * jnp.sum(parts.astype(F32), axis=0)
    return share, share.astype(BF16)


def final_body(gathered, out):
    size, _, rows, bond = gathered.shape
    total = jnp.zeros((rows, bond), F32)
    for q in range(size):
        for x in range(4):
            value = gathered[q, x].astype(F32)
            total = total + value * value
    mean = jnp.sum(total) / (size * 4 * rows * bond)
    scale = lax.rsqrt(jnp.full((8, 128), mean + EPS, F32))[0:1, 0:1]
    halves = bond // 128
    pitch = 4 * halves
    for q in range(size):
        for x in range(4):
            value = gathered[q, x].astype(F32) * scale
            s, t = x // 2, x % 2
            for j in range(halves):
                begin = q * rows * pitch + s * 2 * halves + j * 2 + t
                out[pl.ds(begin, rows, stride=pitch), :] = value[:, j * 128 : (j + 1) * 128]


def final_call(gathered):
    size, _, rows, bond = gathered.shape
    halves = bond // 128
    flat = call(
        final_body,
        jax.ShapeDtypeStruct((size * rows * 4 * halves, 128), F32),
        [VMEM],
        nbytes=gathered.size * 6,
    )(gathered)[0]
    blocks = flat.reshape(size * rows, 2, halves, 2, 128)
    return jnp.transpose(blocks, (0, 1, 3, 2, 4)).reshape(1, size * rows, 2, 2, bond)


def levels_first(site):
    return jnp.transpose(site, (1, 0, 2))


def shards(meet_env, meet_iso, last_site, first_site, term_kind):
    sections, size = lax.axis_size("sec"), lax.axis_size("term")
    own_env = meet_env[0]
    section = lax.axis_index("sec")
    odd = section % 2
    far = (section % (sections // 2) == 0).astype(jnp.int32)
    facts = jnp.stack([odd, lax.axis_index("term"), far])
    facts = jnp.concatenate([facts.astype(jnp.int32), term_kind[:, 0], term_kind[:, 1]])
    bond = own_env.shape[1]

    swap = [(i, i ^ 1) for i in range(sections)]
    to_odd = [(i, i + 1) for i in range(0, sections, 2)]
    onward = [(i, (i + 1) % sections) for i in range(sections)]
    odd_on = [(i, (i + 1) % sections) for i in range(1, sections, 2)]

    half = sections // 2
    row = min(ROW, half)
    ends = [half - 1, sections - 1]
    by_row = [(i, j) for i, j in odd_on if i not in ends] + [(i, i - half + row) for i in ends]
    then_on = [(i - half + row, (i + 1) % sections) for i in ends]

    own_iso = levels_first(meet_iso[0])
    own_last = levels_first(last_site[0])
    once = extend_call(extend_first_body, facts, own_env, own_iso)
    raw_env, once = lax.optimization_barrier((own_env, once))
    once = lax.ppermute(once, "sec", swap)
    partner = lax.ppermute(raw_env, "sec", to_odd)
    last = lax.ppermute(own_last, "sec", onward)
    fresh = extend_call(extend_odd_body, facts, once, own_iso)
    cut = CUT * bond // 16
    came = lax.ppermute(fresh[:, :cut], "sec", odd_on)
    piece = lax.ppermute(fresh[:, cut:], "sec", by_row)
    relayed = lax.ppermute(piece, "sec", then_on)
    first = levels_first(first_site[0])
    applied, share, summand, right_env = first_call(
        size, facts, last, first, own_env, partner, once, own_iso
    )
    summand, left_env = second_call(
        facts, applied, summand, partner, came, piece, relayed
    )
    parts = lax.all_to_all(summand, "term", 0, 0, tiled=True)
    share, rounded = update(parts, share)
    gathered = lax.all_gather(rounded, "term")
    summand = apply_call(facts, gathered, left_env, right_env)
    parts = lax.all_to_all(summand, "term", 0, 0, tiled=True)
    share, rounded = update(parts, share)
    copies = jnp.broadcast_to(rounded, (size, *rounded.shape))
    gathered = lax.all_to_all(copies, "term", 0, 0, tiled=True)
    return final_call(gathered)


def solution(mesh):
    in_specs = (
        P("sec", "term", None, None),
        P("sec", None, None, None),
        P("sec", None, None, None),
        P("sec", None, None, None),
        P("term", None),
    )
    out_specs = P("sec", None, None, None, None)
    return jax.shard_map(shards, mesh=mesh, in_specs=in_specs, out_specs=out_specs, check_vma=False)
```
